32 devices in a mesh: dom: 8 (over z, x), band: 4 (over y, core).
Axes of the slice: x: 2, y: 2, z: 4, core: 2. Of those that a mesh axis runs over, the one named last changes fastest.
Arguments:
- states: float32 [160, 48, 3584], P('band', 'dom'), may hold values from -6 to 6
- potential: float32 [48, 3584], P('dom'), may hold values from -4 to 1
- counts: int32 [4], replicated, may hold values from 1 to 40, 128 in all
Outputs:
- filtered: float32 [160, 48, 3584], P('band', 'dom')
- projected: float32 [2, 160, 160], P(None, 'band', 'dom')
The draws below stay inside these ranges and needn't reach their ends.
Inputs may be any that keep to these rules, and one draw needn't show every extreme that they name: The counts sum to 128; the largest equals 40.
All inputs are finite; a program needn't handle non-finite values.
Results may differ from the reference program's by a relative error of at most 0.000057.
Values sent between devices are 32-bit elements; how exact they have to be, the bound alone decides.
A program may use at most 128 MiB of HBM per device.

```python
import math
import jax
import jax.numpy as jnp
import numpy as np
from jax import lax

BCAP = 40
STATES = 128
SLOTS = 160
NY = 56
NZ = 64
NX = 48
N_BAND = 4


def steps_of(rng, shape, shards, least, top_value):
    gain, own = 1.0, jax.random.fold_in(rng, 6)
    for axis_at, parts in shards:
        heights = jnp.exp(jax.random.uniform(jax.random.fold_in(own, axis_at), (parts,), jnp.float32, least / len(shards), top_value / len(shards)))
        gain = gain * jnp.repeat(heights, shape[axis_at] // parts).reshape([-1 if axis == axis_at else 1 for axis in range(len(shape))])
    return gain


def length_profile(number_of, total, most, slope):
    weights = [(1 << 20) // math.isqrt(standing ** slope) + 1 for standing in range(2, number_of + 1)]
    surplus, given = total - most - (number_of - 1), [1] * (number_of - 1)
    while surplus > 0:
        movable = [i for i in range(number_of - 1) if given[i] < most]
        whole, remaining = sum([weights[i] for i in movable]), surplus
        for i in movable:
            addition = min(most - given[i], max(1, remaining * weights[i] // whole), surplus)
            given[i] = given[i] + addition
            surplus = surplus - addition
    return np.array([most] + given)


def uneven_parts(own_key, number_of, total, limit, skew):
    if number_of == 2:
        one = jax.random.randint(own_key, (), max(1, total - limit), min(limit, total - 1) + 1)
        return jnp.stack([one, total - one])
    sizes = jnp.asarray(length_profile(number_of, total, limit, skew), jnp.int32)
    couples = (number_of - 1) // 2
    source_of, receiver = sizes[1:1 + 2 * couples:2], sizes[2:2 + 2 * couples:2]
    slack = jnp.minimum(source_of - 1, limit - receiver)
    shifted = jax.random.randint(jax.random.fold_in(own_key, 1), (couples,), 0, 1 << 20) % (slack + 1)
    sizes = sizes.at[1:1 + 2 * couples:2].set(source_of - shifted).at[2:2 + 2 * couples:2].set(receiver + shifted)
    return sizes[jax.random.permutation(jax.random.fold_in(own_key, 2), number_of)]


def scatter_about(stream_key, shape, width, reach, shards=(), held_as=jnp.bfloat16):
    level = steps_of(stream_key, shape, shards, -0.22, 0.18) if shards else 1.0
    entries = jax.random.normal(stream_key, shape, jnp.float32) * width * level
    return jnp.minimum(jnp.maximum(entries, -reach), reach).astype(held_as)


def setup_inputs(seed: int = 0) -> dict:
    keys = jax.random.split(jax.random.key(seed), 4)
    states = scatter_about(keys[0], (SLOTS, NX, NY * NZ), 1.0, 6.0, ((0, 4), (1, 8)), jnp.float32)
    potential = jnp.clip(-4.0 + 5.0 * jax.random.uniform(keys[1], (NX, NY * NZ), jnp.float32) ** steps_of(keys[1], (NX, NY * NZ), ((0, 8),), -0.2, 0.2), -4.0, 1.0)
    counts = uneven_parts(keys[2], N_BAND, STATES, BCAP, 2).astype(jnp.int32)
    return {"states": states, "potential": potential, "counts": counts}


def stencil_weights():
    fact = math.factorial
    sides = [2.0 * (-1.0) ** (k + 1) * fact(6) ** 2 / (k * k * fact(6 - k) * fact(6 + k)) for k in range(1, 7)]
    return -2.0 * sum(sides), sides


def apply_hamiltonian(field, potential):
    center_weight, side_weights = stencil_weights()
    span_x, span_y, span_z = field.shape[1], field.shape[2], field.shape[3]
    padded = jnp.pad(field, ((0, 0), (6, 6), (6, 6), (6, 6)))
    total = 3.0 * center_weight * field
    for step in range(1, 7):
        factor = side_weights[step - 1]
        near = padded[:, 6 + step:6 + step + span_x, 6:6 + span_y, 6:6 + span_z]
        near = near + padded[:, 6 - step:6 - step + span_x, 6:6 + span_y, 6:6 + span_z]
        near = near + padded[:, 6:6 + span_x, 6 + step:6 + step + span_y, 6:6 + span_z]
        near = near + padded[:, 6:6 + span_x, 6 - step:6 - step + span_y, 6:6 + span_z]
        near = near + padded[:, 6:6 + span_x, 6:6 + span_y, 6 + step:6 + step + span_z]
        near = near + padded[:, 6:6 + span_x, 6:6 + span_y, 6 - step:6 - step + span_z]
        total = total + factor * near
    return potential[None] * field - 0.5 * (1.0 / 0.36) * total


def reference(states, potential, counts):
    slot_ids = jnp.arange(BCAP, dtype=jnp.int32)
    keep = (slot_ids[None, :] < counts[:, None]).astype(jnp.float32).reshape(SLOTS)
    grid_states = states.reshape(SLOTS, NX, NY, NZ)
    grid_potential = potential.reshape(NX, NY, NZ)
    start = grid_states * keep[:, None, None, None]
    first = (apply_hamiltonian(start, grid_potential) - 11.0 * start) / 11.0
    second = 2.0 * (apply_hamiltonian(first, grid_potential) - 11.0 * first) / 11.0 - start
    filtered = 2.0 * (apply_hamiltonian(second, grid_potential) - 11.0 * second) / 11.0 - first
    image = apply_hamiltonian(filtered, grid_potential)
    flat_states = filtered.reshape(SLOTS, -1)
    flat_image = image.reshape(SLOTS, -1)
    intersection = jnp.dot(flat_states, flat_states.T, preferred_element_type=jnp.float32, precision=lax.Precision.HIGHEST)
    hamilton = jnp.dot(flat_image, flat_states.T, preferred_element_type=jnp.float32, precision=lax.Precision.HIGHEST)
    return filtered.reshape(SLOTS, NX, NY * NZ), jnp.stack([intersection, hamilton])
```

```python
import functools
import math

import jax
import jax.numpy as jnp
import ml_dtypes
import numpy as np
from jax import lax
from jax.experimental import pallas as pl
from jax.experimental.pallas import tpu as pltpu
from jax.sharding import PartitionSpec as P

NY = 56
NZ = 64
REACH = 6
LANES = 256
EDGE = REACH * NZ
VMEM_BYTES = 60 * 1024 * 1024


def stencil_weights():
    fact = math.factorial
    sides = [
        2.0 * (-1.0) ** (k + 1) * fact(6) ** 2 / (k * k * fact(6 - k) * fact(6 + k))
        for k in range(1, 7)
    ]
    return (-2.0 * sum(sides), sides)


CENTER, SIDES = stencil_weights()
SCALE = -0.5 * (1.0 / 0.36)


def side_table(distance):
    table = np.zeros(distance.shape, np.float64)
    for step in range(1, REACH + 1):
        table += np.where(np.abs(distance) == step, SCALE * SIDES[step - 1], 0.0)
    return table


def halves(table):
    high = table.astype(ml_dtypes.bfloat16)
    low = (table - high.astype(np.float64)).astype(ml_dtypes.bfloat16)
    return np.stack([high, low])


def plane_matrix():
    k = np.arange(LANES + 2 * EDGE)[:, None] - EDGE
    n = np.arange(LANES)[None, :]
    dy = k // NZ - n // NZ
    dz = k % NZ - n % NZ
    return halves(np.where(dz == 0, side_table(dy), 0.0) + np.where(dy == 0, side_table(dz), 0.0))


def row_table(parts, each, planes, rows):
    r = np.arange(parts * rows)
    source, inner = r // rows, r % rows
    valid = inner < each * planes
    slot = np.where(valid, inner // planes, -1)
    return source, slot, inner % planes, valid


def cross_matrix(parts, each, planes, rows):
    source, slot, plane, valid = row_table(parts, each, planes, rows)
    x = source * planes + plane
    same = (slot[:, None] == slot[None, :]) & valid[:, None] & valid[None, :]
    return halves(np.where(same, side_table(x[:, None] - x[None, :]), 0.0))


def spread_matrix(parts, each, planes, rows):
    source, slot, plane, valid = row_table(parts, each, planes, rows)
    x = source * planes + plane
    return ((x[:, None] == np.arange(parts * planes)[None, :]) & valid[:, None]).astype(np.float32)


def split(value):
    high = value.astype(jnp.bfloat16)
    return high, (value - high.astype(jnp.float32)).astype(jnp.bfloat16)


def dot3(left_high, left_low, right_high, right_low):
    dot = functools.partial(jnp.dot, preferred_element_type=jnp.float32)
    return dot(left_high, right_high) + (dot(left_high, right_low) + dot(left_low, right_high))


def filter_kernel(start, potential, spread, near, cross, filtered, image, field, held, first, second):
    cells = start.shape[1]
    chunks = cells // LANES
    rows = start.shape[0]
    for part in range(2):
        for half in range(2):
            held[part, half, :, 0:EDGE] = jnp.zeros((rows, EDGE), jnp.bfloat16)
            held[part, half, :, EDGE + cells :] = jnp.zeros((rows, EDGE), jnp.bfloat16)

    def keep(part, c, value):
        at = pl.ds(pl.multiple_of(c * LANES + EDGE, 128), LANES)
        high, low = split(value)
        held[part, 0, :, at] = high
        held[part, 1, :, at] = low

    @pl.loop(0, chunks)
    def _(c):
        at = pl.ds(pl.multiple_of(c * LANES, 128), LANES)
        field[:, at] = jnp.dot(
            spread[...], potential[:, at], precision=lax.Precision.HIGHEST, preferred_element_type=jnp.float32
        ) + 3.0 * CENTER * SCALE
        keep(0, c, start[:, at])

    def apply(part, now, before, out, gain, own, last):
        @pl.loop(0, chunks)
        def _(c):
            at = pl.ds(pl.multiple_of(c * LANES, 128), LANES)
            wide = pl.ds(pl.multiple_of(c * LANES, 128), LANES + 2 * EDGE)
            mid = pl.ds(pl.multiple_of(c * LANES + EDGE, 128), LANES)
            total = dot3(held[part, 0, :, wide], held[part, 1, :, wide], near[0], near[1])
            total += dot3(cross[0], cross[1], held[part, 0, :, mid], held[part, 1, :, mid])
            value = now[:, at]
            result = gain * (field[:, at] * value + total) + own * value
            if before is not None:
                result = result - before[:, at]
            out[:, at] = result
            if not last:
                keep(1 - part, c, result)

    apply(0, start, None, first, 1.0 / 11.0, -1.0, False)
    apply(1, first, start, second, 2.0 / 11.0, -2.0, False)
    apply(0, second, first, filtered, 2.0 / 11.0, -2.0, False)
    apply(1, filtered, None, image, 1.0, 0.0, True)


def run_filter(start, potential, parts, each, planes, rows):
    total, cells = start.shape
    spread = jnp.asarray(spread_matrix(parts, each, planes, rows))
    near = jnp.asarray(plane_matrix())
    cross = jnp.asarray(cross_matrix(parts, each, planes, rows))
    shape = jax.ShapeDtypeStruct((total, cells), jnp.float32)
    work = pltpu.VMEM((total, cells), jnp.float32)
    return pl.pallas_call(
        filter_kernel,
        out_shape=(shape, shape),
        in_specs=[pl.BlockSpec(memory_space=pltpu.VMEM)] * 5,
        out_specs=(pl.BlockSpec(memory_space=pltpu.VMEM),) * 2,
        scratch_shapes=[work, pltpu.VMEM((2, 2, total, cells + 2 * EDGE), jnp.bfloat16), work, work],
        compiler_params=pltpu.CompilerParams(vmem_limit_bytes=VMEM_BYTES),
        name="filter_states",
    )(start, potential, spread, near, cross)


def gram_kernel(own, image, every, same, fold_left, fold_right, out, total):
    step = pl.program_id(0)

    @pl.when(step == 0)
    def _():
        total[...] = jnp.zeros_like(total)

    every_high, every_low = split(every[...])
    dot = functools.partial(
        lax.dot_general, dimension_numbers=(((1,), (1,)), ((), ())), preferred_element_type=jnp.float32
    )
    for which, ref in enumerate((own, image)):
        high, low = split(ref[...])
        total[which] += dot(high, every_high) + (dot(high, every_low) + dot(low, every_high))

    @pl.when(step == pl.num_programs(0) - 1)
    def _():
        exact = functools.partial(
            jnp.dot, precision=lax.Precision.HIGHEST, preferred_element_type=jnp.float32
        )
        for which in range(2):
            out[which] = exact(exact(fold_left[...], total[which] * same[...]), fold_right[...])


def run_gram(own, image, every, parts, each, planes, rows, capacity, bands):
    total, cells = own.shape
    width = every.shape[0]
    source, slot, plane, valid = row_table(parts, each, planes, rows)
    index = source * each + slot
    fold = ((index[None, :] == np.arange(capacity)[:, None]) & valid[None, :]).astype(np.float32)
    plane = np.where(valid, plane, -1)
    same = (plane[:, None] == np.tile(plane, bands)[None, :]).astype(np.float32)
    fold_right = np.kron(np.eye(bands, dtype=np.float32), fold.T)
    block = pl.BlockSpec((total, LANES), lambda i: (0, i))
    return pl.pallas_call(
        gram_kernel,
        grid=(cells // LANES,),
        out_shape=jax.ShapeDtypeStruct((2, capacity, bands * capacity), jnp.float32),
        in_specs=[
            block,
            block,
            pl.BlockSpec((width, LANES), lambda i: (0, i)),
            pl.BlockSpec(memory_space=pltpu.VMEM),
            pl.BlockSpec(memory_space=pltpu.VMEM),
            pl.BlockSpec(memory_space=pltpu.VMEM),
        ],
        out_specs=pl.BlockSpec((2, capacity, bands * capacity), lambda i: (0, 0, 0)),
        scratch_shapes=[pltpu.VMEM((2, total, width), jnp.float32)],
        compiler_params=pltpu.CompilerParams(vmem_limit_bytes=VMEM_BYTES),
        name="gram",
    )(own, image, every, jnp.asarray(same), jnp.asarray(fold), jnp.asarray(fold_right))


def local(states, potential, counts):
    capacity, planes, cells = states.shape
    parts, bands = lax.axis_size("dom"), lax.axis_size("band")
    each = -(-capacity // parts)
    rows = -(-each * planes // 8) * 8
    live_count = counts[lax.axis_index("band")]
    keep = (jnp.arange(capacity, dtype=jnp.int32) < live_count).astype(jnp.float32)
    start = states * keep[:, None, None]
    start = jnp.pad(start, ((0, parts * each - capacity), (0, 0), (0, 0)))
    start = start.reshape(parts, each * planes, cells)
    start = jnp.pad(start, ((0, 0), (0, rows - each * planes), (0, 0)))
    whole_potential = lax.all_gather(potential, "dom", axis=0, tiled=True)
    start = lax.all_to_all(start, "dom", 0, 0, tiled=True).reshape(parts * rows, cells)
    filtered, image = run_filter(start, whole_potential, parts, each, planes, rows)
    back = lambda a: lax.all_to_all(a.reshape(parts, rows, cells), "dom", 0, 0, tiled=True).reshape(parts * rows, cells)
    filtered = back(filtered)
    every = lax.all_gather(filtered, "band", axis=0, tiled=True)
    image = back(image)
    terms = run_gram(filtered, image, every, parts, each, planes, rows, capacity, bands)
    projected = lax.psum_scatter(terms, "dom", scatter_dimension=2, tiled=True)
    result = filtered.reshape(parts, rows, cells)[:, : each * planes]
    result = result.reshape(parts * each, planes, cells)[:capacity]
    return result, projected


def solution(mesh):
    return jax.shard_map(
        local,
        mesh=mesh,
        in_specs=(P("band", "dom", None), P("dom", None), P()),
        out_specs=(P("band", "dom", None), P(None, "band", "dom")),
        check_vma=False,
    )
```

```python
import functools
import math

import jax
import jax.numpy as jnp
import ml_dtypes
import numpy as np
from jax import lax
from jax.experimental import pallas as pl
from jax.experimental.pallas import tpu as pltpu
from jax.sharding import PartitionSpec as P

NY = 56
NZ = 64
REACH = 6
LANES = 256
EDGE = REACH * NZ
VMEM_BYTES = 62 * 1024 * 1024


def stencil_weights():
    fact = math.factorial
    sides = [
        2.0 * (-1.0) ** (k + 1) * fact(6) ** 2 / (k * k * fact(6 - k) * fact(6 + k))
        for k in range(1, 7)
    ]
    return (-2.0 * sum(sides), sides)


CENTER, SIDES = stencil_weights()
SCALE = -0.5 * (1.0 / 0.36)


def side_table(distance):
    table = np.zeros(distance.shape, np.float64)
    for step in range(1, REACH + 1):
        table += np.where(np.abs(distance) == step, SCALE * SIDES[step - 1], 0.0)
    return table


def halves(table):
    high = table.astype(ml_dtypes.bfloat16)
    low = (table - high.astype(np.float64)).astype(ml_dtypes.bfloat16)
    return np.stack([high, low])


def plane_matrix():
    k = np.arange(LANES + 2 * EDGE)[:, None] - EDGE
    n = np.arange(LANES)[None, :]
    dy = k // NZ - n // NZ
    dz = k % NZ - n % NZ
    return halves(np.where(dz == 0, side_table(dy), 0.0) + np.where(dy == 0, side_table(dz), 0.0))


def packed_rows(each, planes):
    r = np.arange(2 * each * planes)
    half, inner = r // (each * planes), r % (each * planes)
    return half, inner // each, inner % each


def cross_matrices(each, planes):
    half, plane, slot = packed_rows(each, planes)
    here = half * planes + plane
    edge = np.where(half == 0, plane - planes, plane + 2 * planes)
    same = slot[:, None] == slot[None, :]
    mid = np.where(same, side_table(here[:, None] - here[None, :]), 0.0)
    out = np.where(same, side_table(here[:, None] - edge[None, :]), 0.0)
    return np.stack([halves(mid), halves(out)])


def spread_matrix(each, planes, tall):
    half, plane, slot = packed_rows(each, planes)
    return ((half * tall + plane)[:, None] == np.arange(2 * tall)[None, :]).astype(np.float32)


def order_matrix(each, planes):
    group, plane, slot = packed_rows(each, planes)
    natural = plane * 2 * each + group * each + slot
    return (natural[:, None] == np.arange(natural.size)[None, :]).astype(ml_dtypes.bfloat16)


def split(value):
    high = value.astype(jnp.bfloat16)
    return high, (value - high.astype(jnp.float32)).astype(jnp.bfloat16)


def dot3(left_high, left_low, right_high, right_low):
    dot = functools.partial(jnp.dot, preferred_element_type=jnp.float32)
    return dot(left_high, right_high) + (dot(left_high, right_low) + dot(left_low, right_high))


def reorder(order, value):
    high = value.astype(jnp.bfloat16)
    rest = value - high.astype(jnp.float32)
    middle = rest.astype(jnp.bfloat16)
    low = (rest - middle.astype(jnp.float32)).astype(jnp.bfloat16)
    dot = functools.partial(jnp.dot, preferred_element_type=jnp.float32)
    return dot(order, high) + (dot(order, middle) + dot(order, low))


def filter_kernel(
    dom_size, band_size, states, potential, live, spread, near, cross, pack, unpack,
    natural, own_filtered, own_image, every,
    fields, given, halo, held, field, shared, gone,
    halo_send, halo_recv, pair_send, pair_recv, pot_sem, core_send, core_recv, far_send, far_recv, on_send, on_recv, own_sem,
):
    cells = states.shape[1]
    chunks = cells // LANES
    rows = states.shape[0]
    block = rows // 2
    dom, band = lax.axis_index("dom"), lax.axis_index("band")
    member = lax.rem(dom, 2)
    partner = dom + 1 - 2 * member
    core = lax.rem(band, 2)
    twin = band + 1 - 2 * core
    place = band // 2
    places = band_size // 2
    has_low, has_high = dom >= 2, dom < dom_size - 2
    far = [2 * lax.rem(place + step, places) + core for step in range(1, places)]
    back = [2 * lax.rem(place + places - step, places) + core for step in range(1, places)]
    whom = lambda **at: dict(device_id=at, device_id_type=pl.DeviceIdType.MESH)

    barrier = pltpu.get_barrier_semaphore()
    pl.semaphore_signal(barrier, inc=1, **whom(dom=partner))
    pl.semaphore_signal(barrier, inc=1, **whom(band=twin))
    for other in far:
        pl.semaphore_signal(barrier, inc=1, **whom(band=other))

    @pl.when(has_low)
    def _():
        pl.semaphore_signal(barrier, inc=1, **whom(dom=dom - 2))

    @pl.when(has_high)
    def _():
        pl.semaphore_signal(barrier, inc=1, **whom(dom=dom + 2))

    pl.semaphore_wait(barrier, 1 + places + has_low.astype(jnp.int32) + has_high.astype(jnp.int32))

    def lanes(c, edge=0, width=LANES):
        return pl.ds(pl.multiple_of(c * LANES + edge, 128), width)

    def remote(source, target, send, recv, **at):
        return pltpu.make_async_remote_copy(source, target, send, recv, **whom(**at))

    def pot_copy():
        return remote(potential, shared.at[member], pot_sem.at[0], pot_sem.at[1], dom=partner)

    def pair_copy(step, c):
        at = lanes(c)
        source = (given, fields.at[3, 1 - member], gone)[step]
        target = (fields.at[0, member], own_filtered.at[member], own_image.at[member])[step]
        return remote(source.at[:, at], target.at[:, at], pair_send.at[step, c], pair_recv.at[step, c], dom=partner)

    def halo_copy(k, side, c, to=None):
        at = lanes(c)
        to = dom + 4 * side - 2 if to is None else to
        return remote(
            fields.at[k, side, :, at], halo.at[k, 1 - side, :, at],
            halo_send.at[k, side, c], halo_recv.at[k, 1 - side, c], dom=to,
        )

    def at_side(side, act):
        pl.when(has_low if side == 0 else has_high)(act)

    def send_halo(k, side, c):
        at_side(side, lambda: halo_copy(k, side, c).start())

    def core_copy(c):
        at = lanes(c)
        return [
            remote(own_filtered.at[g, :, at], every.at[band, g, :, at], core_send.at[g, c], core_recv.at[g, c], band=twin)
            for g in range(2)
        ]

    def far_copy(step, c):
        at = lanes(c)
        return [
            remote(
                own_filtered.at[g, :, at], every.at[band, g, :, at],
                far_send.at[step, g, c], far_recv.at[step, g, c], band=far[step],
            )
            for g in range(2)
        ]

    def on_copy(step, c):
        at = lanes(c)
        return [
            remote(
                every.at[back[step], g, :, at], every.at[back[step], g, :, at],
                on_send.at[step, g, c], on_recv.at[step, g, c], band=twin,
            )
            for g in range(2)
        ]

    def own_copy(c):
        at = lanes(c)
        return [
            pltpu.make_async_copy(own_filtered.at[g, :, at], every.at[band, g, :, at], own_sem.at[g, c])
            for g in range(2)
        ]

    def keep(part, c, value):
        at = lanes(c, EDGE)
        high, low = split(value)
        held[part, 0, :, at] = high
        held[part, 1, :, at] = low

    pot_copy().start()
    shared[member] = potential[...]
    for part in range(2):
        for half in range(2):
            held[part, half, :, 0:EDGE] = jnp.zeros((rows, EDGE), jnp.bfloat16)
            held[part, half, :, EDGE + cells :] = jnp.zeros((rows, EDGE), jnp.bfloat16)

    @pl.loop(0, chunks)
    def _(c):
        at = lanes(c)
        packed = reorder(pack[...], states[:, at]) * live[...]
        first, second = packed[:block], packed[block:]
        fields[0, member, :, at] = jnp.where(member == 0, first, second)
        given[:, at] = jnp.where(member == 0, second, first)
        pair_copy(0, c).start()
        for side in range(2):
            pl.when(member == side)(lambda side=side: send_halo(0, side, c))

        @pl.when(jnp.logical_not(has_low))
        def _():
            for k in range(4):
                halo[k, 0, :, at] = jnp.zeros((block, LANES), jnp.float32)

        @pl.when(jnp.logical_not(has_high))
        def _():
            for k in range(4):
                halo[k, 1, :, at] = jnp.zeros((block, LANES), jnp.float32)

    pot_copy().wait()

    def arrive(c):
        at = lanes(c)
        pair_copy(0, c).wait_recv()
        for side in range(2):
            pl.when(member == 1 - side)(lambda side=side: send_halo(0, side, c))
        keep(0, c, jnp.concatenate([fields[0, 0, :, at], fields[0, 1, :, at]], axis=0))
        pots = jnp.concatenate([shared[0, :, at], shared[1, :, at]], axis=0)
        field[:, at] = jnp.dot(
            spread[...], pots, precision=lax.Precision.HIGHEST, preferred_element_type=jnp.float32
        ) + 3.0 * CENTER * SCALE

    def gather(c):
        at = lanes(c)
        pair_copy(1, c).wait_recv()
        for step in range(places - 1):
            for copy in far_copy(step, c):
                copy.start()
        for copy in core_copy(c) + own_copy(c):
            copy.start()
        both = jnp.concatenate([own_filtered[0, :, at], own_filtered[1, :, at]], axis=0)
        natural[:, at] = reorder(unpack[...], both)

    def forward(c):
        for step in range(places - 1):
            for copy in far_copy(step, c):
                copy.wait_recv()
            for copy in on_copy(step, c):
                copy.start()

    def apply(k, c, gain, own):
        at = lanes(c)
        part = k % 2
        for side in range(2):
            at_side(side, lambda side=side: halo_copy(k, 1 - side, c, partner).wait_recv())
        wide, mid = lanes(c, 0, LANES + 2 * EDGE), lanes(c, EDGE)
        total = dot3(held[part, 0, :, wide], held[part, 1, :, wide], near[0], near[1])
        total += dot3(cross[0, 0], cross[0, 1], held[part, 0, :, mid], held[part, 1, :, mid])
        out_high, out_low = split(jnp.concatenate([halo[k, 0, :, at], halo[k, 1, :, at]], axis=0))
        total += dot3(cross[1, 0], cross[1, 1], out_high, out_low)
        value = jnp.concatenate([fields[k, 0, :, at], fields[k, 1, :, at]], axis=0)
        result = gain * (field[:, at] * value + total) + own * value
        if k in (1, 2):
            result = result - jnp.concatenate([fields[k - 1, 0, :, at], fields[k - 1, 1, :, at]], axis=0)
        if k < 3:
            fields[k + 1, 0, :, at] = result[:block]
            fields[k + 1, 1, :, at] = result[block:]
            for side in range(2):
                send_halo(k + 1, side, c)
            keep(1 - part, c, result)
        return result

    for c in range(2):
        arrive(c)

    @pl.loop(0, chunks)
    def _(c):
        pl.when(c + 2 < chunks)(lambda: arrive(c + 2))
        apply(0, c, 1.0 / 11.0, -1.0)

    @pl.loop(0, chunks)
    def _(c):
        apply(1, c, 2.0 / 11.0, -2.0)

    @pl.loop(0, chunks)
    def _(c):
        at = lanes(c)
        result = apply(2, c, 2.0 / 11.0, -2.0)
        pair_copy(1, c).start()
        own_filtered[member, :, at] = jnp.where(member == 0, result[:block], result[block:])
        pl.when(c >= 2)(lambda: gather(c - 2))

    pl.loop(chunks - 2, chunks)(gather)
    lag = 4

    @pl.loop(0, chunks)
    def _(c):
        at = lanes(c)
        result = apply(3, c, 1.0, 0.0)
        own_image[member, :, at] = jnp.where(member == 0, result[:block], result[block:])
        gone[:, at] = jnp.where(member == 0, result[block:], result[:block])
        pair_copy(2, c).start()
        pl.when(c >= lag)(lambda: forward(c - lag))

    pl.loop(chunks - lag, chunks)(forward)

    @pl.loop(0, chunks)
    def _(c):
        pair_copy(2, c).wait_recv()
        for step in range(3):
            pair_copy(step, c).wait_send()
        for k in range(4):
            for side in range(2):
                at_side(side, lambda k=k, side=side: halo_copy(k, side, c).wait_send())
        for copy in core_copy(c):
            copy.wait()
        for copy in own_copy(c):
            copy.wait()
        for step in range(places - 1):
            for copy in far_copy(step, c):
                copy.wait_send()
            for copy in on_copy(step, c):
                copy.wait()


def run_filter(states, potential, live, each, planes, dom_size, band_size):
    rows, cells = states.shape
    block, chunks, tall = rows // 2, cells // LANES, potential.shape[0]
    order = order_matrix(each, planes)
    f32 = lambda *shape: pltpu.VMEM(shape, jnp.float32)
    dma = lambda *shape: pltpu.SemaphoreType.DMA(shape)
    out = lambda *shape: jax.ShapeDtypeStruct(shape, jnp.float32)
    others = max(band_size // 2 - 1, 1)
    vmem = pl.BlockSpec(memory_space=pltpu.VMEM)
    return pl.pallas_call(
        functools.partial(filter_kernel, dom_size, band_size),
        out_shape=(
            out(rows, cells), out(2, block, cells), out(2, block, cells), out(band_size, 2, block, cells),
        ),
        in_specs=[vmem] * 8,
        out_specs=(vmem, vmem, vmem, pl.BlockSpec(memory_space=pl.ANY)),
        scratch_shapes=[
            f32(4, 2, block, cells), f32(block, cells), f32(4, 2, block, cells),
            pltpu.VMEM((2, 2, rows, cells + 2 * EDGE), jnp.bfloat16),
            f32(rows, cells), f32(2, tall, cells), f32(block, cells),
            dma(4, 2, chunks), dma(4, 2, chunks), dma(3, chunks), dma(3, chunks), dma(2),
            dma(2, chunks), dma(2, chunks), dma(others, 2, chunks), dma(others, 2, chunks),
            dma(others, 2, chunks), dma(others, 2, chunks), dma(2, chunks),
        ],
        compiler_params=pltpu.CompilerParams(
            vmem_limit_bytes=VMEM_BYTES, collective_id=0, has_side_effects=True
        ),
        name="filter_states",
    )(
        states, potential, live, jnp.asarray(spread_matrix(each, planes, tall)), jnp.asarray(plane_matrix()),
        jnp.asarray(cross_matrices(each, planes)), jnp.asarray(order), jnp.asarray(order.T),
    )


def gram_kernel(own, image, every, same, fold_left, fold_right, out, total):
    step = pl.program_id(0)

    @pl.when(step == 0)
    def _():
        total[...] = jnp.zeros_like(total)

    every_high, every_low = split(every[...])
    dot = functools.partial(
        lax.dot_general, dimension_numbers=(((1,), (1,)), ((), ())), preferred_element_type=jnp.float32
    )
    for which, ref in enumerate((own, image)):
        high, low = split(ref[...])
        total[which] += dot(high, every_high) + (dot(high, every_low) + dot(low, every_high))

    @pl.when(step == pl.num_programs(0) - 1)
    def _():
        exact = functools.partial(
            jnp.dot, precision=lax.Precision.HIGHEST, preferred_element_type=jnp.float32
        )
        for which in range(2):
            out[which] = exact(exact(fold_left[...], total[which] * same[...]), fold_right[...])


def run_gram(own, image, every, each, planes, capacity, bands):
    total, cells = own.shape
    width = every.shape[0]
    group, plane, slot = packed_rows(each, planes)
    index = group * each + slot
    fold = (index[None, :] == np.arange(capacity)[:, None]).astype(np.float32)
    same = (plane[:, None] == np.tile(plane, bands)[None, :]).astype(np.float32)
    fold_right = np.kron(np.eye(bands, dtype=np.float32), fold.T)
    block = pl.BlockSpec((total, LANES), lambda i: (0, i))
    return pl.pallas_call(
        gram_kernel,
        grid=(cells // LANES,),
        out_shape=jax.ShapeDtypeStruct((2, capacity, bands * capacity), jnp.float32),
        in_specs=[
            block,
            block,
            pl.BlockSpec((width, LANES), lambda i: (0, i)),
            pl.BlockSpec(memory_space=pltpu.VMEM),
            pl.BlockSpec(memory_space=pltpu.VMEM),
            pl.BlockSpec(memory_space=pltpu.VMEM),
        ],
        out_specs=pl.BlockSpec((2, capacity, bands * capacity), lambda i: (0, 0, 0)),
        scratch_shapes=[pltpu.VMEM((2, total, width), jnp.float32)],
        compiler_params=pltpu.CompilerParams(vmem_limit_bytes=VMEM_BYTES),
        name="gram",
    )(own, image, every, jnp.asarray(same), jnp.asarray(fold), jnp.asarray(fold_right))


def local(states, potential, counts):
    capacity, planes, cells = states.shape
    dom_size, bands = lax.axis_size("dom"), lax.axis_size("band")
    each = capacity // 2
    rows = capacity * planes
    live_count = counts[lax.axis_index("band")]
    group, plane, slot = packed_rows(each, planes)
    live = (jnp.asarray(group * each + slot, jnp.int32) < live_count).astype(jnp.float32)[:, None]
    tall_potential = jnp.pad(potential, ((0, -planes % 8), (0, 0)))
    natural, filtered, image, every = run_filter(
        states.transpose(1, 0, 2).reshape(rows, cells), tall_potential, live, each, planes, dom_size, bands
    )
    terms = run_gram(
        filtered.reshape(rows, cells), image.reshape(rows, cells), every.reshape(bands * rows, cells),
        each, planes, capacity, bands,
    )
    projected = lax.psum_scatter(terms, "dom", scatter_dimension=2, tiled=True)
    return natural.reshape(planes, capacity, cells).transpose(1, 0, 2), projected


def solution(mesh):
    return jax.shard_map(
        local,
        mesh=mesh,
        in_specs=(P("band", "dom", None), P("dom", None), P()),
        out_specs=(P("band", "dom", None), P(None, "band", "dom")),
        check_vma=False,
    )
```

```python
import functools
import math

import jax
import jax.numpy as jnp
import ml_dtypes
import numpy as np
from jax import lax
from jax.experimental import pallas as pl
from jax.experimental.pallas import tpu as pltpu
from jax.sharding import PartitionSpec as P

NY = 56
NZ = 64
REACH = 6
LANES = 256
EDGE = REACH * NZ
VMEM_BYTES = 62 * 1024 * 1024


def stencil_weights():
    fact = math.factorial
    sides = [
        2.0 * (-1.0) ** (k + 1) * fact(6) ** 2 / (k * k * fact(6 - k) * fact(6 + k))
        for k in range(1, 7)
    ]
    return (-2.0 * sum(sides), sides)


CENTER, SIDES = stencil_weights()
SCALE = -0.5 * (1.0 / 0.36)


def side_table(distance):
    table = np.zeros(distance.shape, np.float64)
    for step in range(1, REACH + 1):
        table += np.where(np.abs(distance) == step, SCALE * SIDES[step - 1], 0.0)
    return table


def halves(table):
    high = table.astype(ml_dtypes.bfloat16)
    low = (table - high.astype(np.float64)).astype(ml_dtypes.bfloat16)
    return np.stack([high, low])


def plane_matrix():
    k = np.arange(LANES + 2 * EDGE)[:, None] - EDGE
    n = np.arange(LANES)[None, :]
    dy = k // NZ - n // NZ
    dz = k % NZ - n % NZ
    return halves(np.where(dz == 0, side_table(dy), 0.0) + np.where(dy == 0, side_table(dz), 0.0))


def packed_rows(each, planes):
    r = np.arange(2 * each * planes)
    half, inner = r // (each * planes), r % (each * planes)
    return half, inner // each, inner % each


def cross_matrices(each, planes):
    half, plane, slot = packed_rows(each, planes)
    here = half * planes + plane
    edge = np.where(half == 0, plane - planes, plane + 2 * planes)
    same = slot[:, None] == slot[None, :]
    mid = np.where(same, side_table(here[:, None] - here[None, :]), 0.0)
    out = np.where(same, side_table(here[:, None] - edge[None, :]), 0.0)
    return np.stack([halves(mid), halves(out)])


def spread_matrix(each, planes, tall):
    half, plane, slot = packed_rows(each, planes)
    return ((half * tall + plane)[:, None] == np.arange(2 * tall)[None, :]).astype(np.float32)


def order_matrix(each, planes):
    group, plane, slot = packed_rows(each, planes)
    natural = plane * 2 * each + group * each + slot
    return (natural[:, None] == np.arange(natural.size)[None, :]).astype(ml_dtypes.bfloat16)


def split(value):
    high = value.astype(jnp.bfloat16)
    return high, (value - high.astype(jnp.float32)).astype(jnp.bfloat16)


def dot3(left_high, left_low, right_high, right_low):
    dot = functools.partial(jnp.dot, preferred_element_type=jnp.float32)
    return dot(left_high, right_high) + (dot(left_high, right_low) + dot(left_low, right_high))


def reorder(order, value):
    high = value.astype(jnp.bfloat16)
    rest = value - high.astype(jnp.float32)
    middle = rest.astype(jnp.bfloat16)
    low = (rest - middle.astype(jnp.float32)).astype(jnp.bfloat16)
    dot = functools.partial(jnp.dot, preferred_element_type=jnp.float32)
    return dot(order, high) + (dot(order, middle) + dot(order, low))


def filter_kernel(
    dom_size, band_size, states, potential, live, spread, near, cross, pack, unpack,
    natural, own_filtered, own_image, every,
    fields, given, halo, held, field, shared, gone,
    halo_send, halo_recv, pair_send, pair_recv, pot_sem, core_send, core_recv, far_send, far_recv, on_send, on_recv, own_sem,
):
    cells = states.shape[1]
    chunks = cells // LANES
    rows = states.shape[0]
    block = rows // 2
    dom, band = lax.axis_index("dom"), lax.axis_index("band")
    member = lax.rem(dom, 2)
    partner = dom + 1 - 2 * member
    core = lax.rem(band, 2)
    twin = band + 1 - 2 * core
    place = band // 2
    places = band_size // 2
    has_low, has_high = dom >= 2, dom < dom_size - 2
    far = [2 * lax.rem(place + step, places) + core for step in range(1, places)]
    back = [2 * lax.rem(place + places - step, places) + core for step in range(1, places)]
    whom = lambda **at: dict(device_id=at, device_id_type=pl.DeviceIdType.MESH)

    barrier = pltpu.get_barrier_semaphore()
    pl.semaphore_signal(barrier, inc=1, **whom(dom=partner))
    pl.semaphore_signal(barrier, inc=1, **whom(band=twin))
    for other in far:
        pl.semaphore_signal(barrier, inc=1, **whom(band=other))

    @pl.when(has_low)
    def _():
        pl.semaphore_signal(barrier, inc=1, **whom(dom=dom - 2))

    @pl.when(has_high)
    def _():
        pl.semaphore_signal(barrier, inc=1, **whom(dom=dom + 2))

    pl.semaphore_wait(barrier, 1 + places + has_low.astype(jnp.int32) + has_high.astype(jnp.int32))

    def lanes(c, edge=0, width=LANES):
        return pl.ds(pl.multiple_of(c * LANES + edge, 128), width)

    def remote(source, target, send, recv, **at):
        return pltpu.make_async_remote_copy(source, target, send, recv, **whom(**at))

    def pot_copy():
        return remote(potential, shared.at[member], pot_sem.at[0], pot_sem.at[1], dom=partner)

    def pair_copy(step, c):
        at = lanes(c)
        source = (given, fields.at[3, 1 - member], gone)[step]
        target = (fields.at[0, member], own_filtered.at[member], own_image.at[member])[step]
        return remote(source.at[:, at], target.at[:, at], pair_send.at[step, c], pair_recv.at[step, c], dom=partner)

    def halo_copy(k, side, c, to=None):
        at = lanes(c)
        to = dom + 4 * side - 2 if to is None else to
        return remote(
            fields.at[k, side, :, at], halo.at[k, 1 - side, :, at],
            halo_send.at[k, side, c], halo_recv.at[k, 1 - side, c], dom=to,
        )

    def at_side(side, act):
        pl.when(has_low if side == 0 else has_high)(act)

    def send_halo(k, side, c):
        at_side(side, lambda: halo_copy(k, side, c).start())

    def core_copy(c):
        at = lanes(c)
        return [
            remote(own_filtered.at[g, :, at], every.at[band, g, :, at], core_send.at[g, c], core_recv.at[g, c], band=twin)
            for g in range(2)
        ]

    def far_copy(step, c):
        at = lanes(c)
        return [
            remote(
                own_filtered.at[g, :, at], every.at[band, g, :, at],
                far_send.at[step, g, c], far_recv.at[step, g, c], band=far[step],
            )
            for g in range(2)
        ]

    def on_copy(step, c):
        at = lanes(c)
        return [
            remote(
                every.at[back[step], g, :, at], every.at[back[step], g, :, at],
                on_send.at[step, g, c], on_recv.at[step, g, c], band=twin,
            )
            for g in range(2)
        ]

    def own_copy(c):
        at = lanes(c)
        return [
            pltpu.make_async_copy(own_filtered.at[g, :, at], every.at[band, g, :, at], own_sem.at[g, c])
            for g in range(2)
        ]

    def keep(part, c, value):
        at = lanes(c, EDGE)
        high, low = split(value)
        held[part, 0, :, at] = high
        held[part, 1, :, at] = low

    pot_copy().start()
    shared[member] = potential[...]
    for part in range(2):
        for half in range(2):
            held[part, half, :, 0:EDGE] = jnp.zeros((rows, EDGE), jnp.bfloat16)
            held[part, half, :, EDGE + cells :] = jnp.zeros((rows, EDGE), jnp.bfloat16)

    @pl.loop(0, chunks)
    def _(c):
        at = lanes(c)
        packed = reorder(pack[...], states[:, at]) * live[...]
        first, second = packed[:block], packed[block:]
        fields[0, member, :, at] = jnp.where(member == 0, first, second)
        given[:, at] = jnp.where(member == 0, second, first)
        pair_copy(0, c).start()

        @pl.when(jnp.logical_not(has_low))
        def _():
            for k in range(4):
                halo[k, 0, :, at] = jnp.zeros((block, LANES), jnp.float32)

        @pl.when(jnp.logical_not(has_high))
        def _():
            for k in range(4):
                halo[k, 1, :, at] = jnp.zeros((block, LANES), jnp.float32)

    pot_copy().wait()

    def arrive(c):
        at = lanes(c)
        pair_copy(0, c).wait_recv()
        for side in range(2):
            send_halo(0, side, c)
        keep(0, c, jnp.concatenate([fields[0, 0, :, at], fields[0, 1, :, at]], axis=0))
        pots = jnp.concatenate([shared[0, :, at], shared[1, :, at]], axis=0)
        field[:, at] = jnp.dot(
            spread[...], pots, precision=lax.Precision.HIGHEST, preferred_element_type=jnp.float32
        ) + 3.0 * CENTER * SCALE

    def gather(c):
        at = lanes(c)
        pair_copy(1, c).wait_recv()
        for step in range(places - 1):
            for copy in far_copy(step, c):
                copy.start()
        for copy in core_copy(c) + own_copy(c):
            copy.start()
        both = jnp.concatenate([own_filtered[0, :, at], own_filtered[1, :, at]], axis=0)
        natural[:, at] = reorder(unpack[...], both)

    def forward(c):
        for step in range(places - 1):
            for copy in far_copy(step, c):
                copy.wait_recv()
            for copy in on_copy(step, c):
                copy.start()

    def apply(k, c, gain, own):
        at = lanes(c)
        part = k % 2
        for side in range(2):
            at_side(side, lambda side=side: halo_copy(k, 1 - side, c, partner).wait_recv())
        wide, mid = lanes(c, 0, LANES + 2 * EDGE), lanes(c, EDGE)
        total = dot3(held[part, 0, :, wide], held[part, 1, :, wide], near[0], near[1])
        total += dot3(cross[0, 0], cross[0, 1], held[part, 0, :, mid], held[part, 1, :, mid])
        out_high, out_low = split(jnp.concatenate([halo[k, 0, :, at], halo[k, 1, :, at]], axis=0))
        total += dot3(cross[1, 0], cross[1, 1], out_high, out_low)
        value = jnp.concatenate([fields[k, 0, :, at], fields[k, 1, :, at]], axis=0)
        result = gain * (field[:, at] * value + total) + own * value
        if k in (1, 2):
            result = result - jnp.concatenate([fields[k - 1, 0, :, at], fields[k - 1, 1, :, at]], axis=0)
        if k < 3:
            fields[k + 1, 0, :, at] = result[:block]
            fields[k + 1, 1, :, at] = result[block:]
            for side in range(2):
                send_halo(k + 1, side, c)
            keep(1 - part, c, result)
        return result

    def third(c):
        result = apply(2, c, 2.0 / 11.0, -2.0)
        own_filtered[member, :, lanes(c)] = jnp.where(member == 0, result[:block], result[block:])
        pair_copy(1, c).start()

    def fourth(c):
        at = lanes(c)
        result = apply(3, c, 1.0, 0.0)
        own_image[member, :, at] = jnp.where(member == 0, result[:block], result[block:])
        gone[:, at] = jnp.where(member == 0, result[block:], result[:block])
        pair_copy(2, c).start()

    for c in range(2):
        arrive(c)

    stages = (
        (-2, arrive),
        (0, lambda c: apply(0, c, 1.0 / 11.0, -1.0)),
        (3, lambda c: apply(1, c, 2.0 / 11.0, -2.0)),
        (6, third),
        (9, fourth),
        (7, gather),
        (8, forward),
    )

    @pl.loop(0, chunks + 9)
    def _(wave):
        for behind, stage in stages:
            c = wave - behind

            @pl.when((c >= 0) & (c < chunks))
            def _(c=c, stage=stage):
                stage(c)

    @pl.loop(0, chunks)
    def _(c):
        pair_copy(2, c).wait_recv()
        for step in range(3):
            pair_copy(step, c).wait_send()
        for k in range(4):
            for side in range(2):
                at_side(side, lambda k=k, side=side: halo_copy(k, side, c).wait_send())
        for copy in core_copy(c):
            copy.wait()
        for copy in own_copy(c):
            copy.wait()
        for step in range(places - 1):
            for copy in far_copy(step, c):
                copy.wait_send()
            for copy in on_copy(step, c):
                copy.wait()


def run_filter(states, potential, live, each, planes, dom_size, band_size):
    rows, cells = states.shape
    block, chunks, tall = rows // 2, cells // LANES, potential.shape[0]
    order = order_matrix(each, planes)
    f32 = lambda *shape: pltpu.VMEM(shape, jnp.float32)
    dma = lambda *shape: pltpu.SemaphoreType.DMA(shape)
    out = lambda *shape: jax.ShapeDtypeStruct(shape, jnp.float32)
    others = max(band_size // 2 - 1, 1)
    vmem = pl.BlockSpec(memory_space=pltpu.VMEM)
    return pl.pallas_call(
        functools.partial(filter_kernel, dom_size, band_size),
        out_shape=(
            out(rows, cells), out(2, block, cells), out(2, block, cells), out(band_size, 2, block, cells),
        ),
        in_specs=[vmem] * 8,
        out_specs=(vmem, vmem, vmem, pl.BlockSpec(memory_space=pl.ANY)),
        scratch_shapes=[
            f32(4, 2, block, cells), f32(block, cells), f32(4, 2, block, cells),
            pltpu.VMEM((2, 2, rows, cells + 2 * EDGE), jnp.bfloat16),
            f32(rows, cells), f32(2, tall, cells), f32(block, cells),
            dma(4, 2, chunks), dma(4, 2, chunks), dma(3, chunks), dma(3, chunks), dma(2),
            dma(2, chunks), dma(2, chunks), dma(others, 2, chunks), dma(others, 2, chunks),
            dma(others, 2, chunks), dma(others, 2, chunks), dma(2, chunks),
        ],
        compiler_params=pltpu.CompilerParams(
            vmem_limit_bytes=VMEM_BYTES, collective_id=0, has_side_effects=True
        ),
        name="filter_states",
    )(
        states, potential, live, jnp.asarray(spread_matrix(each, planes, tall)), jnp.asarray(plane_matrix()),
        jnp.asarray(cross_matrices(each, planes)), jnp.asarray(order), jnp.asarray(order.T),
    )


def gram_kernel(dom_size, own, image, every, same, fold_left, fold_right, pick, out, total, mine, theirs, send, recv):
    step = pl.program_id(0)
    rows = own.shape[0]
    dom = lax.axis_index("dom")
    barrier = pltpu.get_barrier_semaphore()

    @pl.when(step == 0)
    def _():
        total[...] = jnp.zeros_like(total)
        for shift in range(1, dom_size):
            pl.semaphore_signal(
                barrier, inc=1, device_id=dict(dom=lax.rem(dom + shift, dom_size)), device_id_type=pl.DeviceIdType.MESH
            )

    every_high, every_low = split(every[...])
    high, low = split(jnp.concatenate([own[...], image[...]], axis=0))
    total[...] += lax.dot_general(
        jnp.concatenate([high, high, low], axis=1),
        jnp.concatenate([every_high, every_low, every_high], axis=1),
        (((1,), (1,)), ((), ())),
        preferred_element_type=jnp.float32,
    )

    @pl.when(step == pl.num_programs(0) - 1)
    def _():
        exact = functools.partial(
            jnp.dot, precision=lax.Precision.HIGHEST, preferred_element_type=jnp.float32
        )
        terms = [
            exact(exact(fold_left[...], total[which * rows : (which + 1) * rows] * same[...]), fold_right[...])
            for which in range(2)
        ]
        pl.semaphore_wait(barrier, dom_size - 1)
        copies = []
        for shift in range(1, dom_size):
            to = lax.rem(dom + shift, dom_size)
            for which in range(2):
                mine[shift, which] = exact(terms[which], pick[to])
            copy = pltpu.make_async_remote_copy(
                mine.at[shift], theirs.at[shift], send.at[shift], recv.at[shift],
                device_id=dict(dom=to), device_id_type=pl.DeviceIdType.MESH,
            )
            copy.start()
            copies.append(copy)
        sums = [exact(terms[which], pick[dom]) for which in range(2)]
        for shift, copy in enumerate(copies, 1):
            copy.wait()
            for which in range(2):
                sums[which] = sums[which] + theirs[shift, which]
        for which in range(2):
            out[which] = sums[which][:, : out.shape[2]]


def run_gram(own, image, every, each, planes, capacity, bands, dom_size):
    total, cells = own.shape
    width = every.shape[0]
    group, plane, slot = packed_rows(each, planes)
    index = group * each + slot
    fold = (index[None, :] == np.arange(capacity)[:, None]).astype(np.float32)
    same = (plane[:, None] == np.tile(plane, bands)[None, :]).astype(np.float32)
    fold_right = np.kron(np.eye(bands, dtype=np.float32), fold.T)
    columns = bands * capacity // dom_size
    lane = np.arange(-(-columns // 128) * 128)
    at = np.arange(dom_size)[:, None, None] * columns + lane[None, None, :]
    pick = ((np.arange(bands * capacity)[None, :, None] == at) & (lane < columns)).astype(np.float32)
    block = pl.BlockSpec((total, 2 * LANES), lambda i: (0, i))
    whole = pl.BlockSpec(memory_space=pltpu.VMEM)
    parcel = pltpu.VMEM((dom_size, 2, capacity, lane.size), jnp.float32)
    return pl.pallas_call(
        functools.partial(gram_kernel, dom_size),
        grid=(cells // (2 * LANES),),
        out_shape=jax.ShapeDtypeStruct((2, capacity, columns), jnp.float32),
        in_specs=[block, block, pl.BlockSpec((width, 2 * LANES), lambda i: (0, i)), whole, whole, whole, whole],
        out_specs=pl.BlockSpec((2, capacity, columns), lambda i: (0, 0, 0)),
        scratch_shapes=[
            pltpu.VMEM((2 * total, width), jnp.float32), parcel, parcel,
            pltpu.SemaphoreType.DMA((dom_size,)), pltpu.SemaphoreType.DMA((dom_size,)),
        ],
        compiler_params=pltpu.CompilerParams(
            vmem_limit_bytes=VMEM_BYTES, collective_id=1, has_side_effects=True
        ),
        name="gram",
    )(own, image, every, jnp.asarray(same), jnp.asarray(fold), jnp.asarray(fold_right), jnp.asarray(pick))


def local(states, potential, counts):
    capacity, planes, cells = states.shape
    dom_size, bands = lax.axis_size("dom"), lax.axis_size("band")
    each = capacity // 2
    rows = capacity * planes
    live_count = counts[lax.axis_index("band")]
    group, plane, slot = packed_rows(each, planes)
    live = (jnp.asarray(group * each + slot, jnp.int32) < live_count).astype(jnp.float32)[:, None]
    tall_potential = jnp.pad(potential, ((0, -planes % 8), (0, 0)))
    natural, filtered, image, every = run_filter(
        states.transpose(1, 0, 2).reshape(rows, cells), tall_potential, live, each, planes, dom_size, bands
    )
    projected = run_gram(
        filtered.reshape(rows, cells), image.reshape(rows, cells), every.reshape(bands * rows, cells),
        each, planes, capacity, bands, dom_size,
    )
    return natural.reshape(planes, capacity, cells).transpose(1, 0, 2), projected


def solution(mesh):
    return jax.shard_map(
        local,
        mesh=mesh,
        in_specs=(P("band", "dom", None), P("dom", None), P()),
        out_specs=(P("band", "dom", None), P(None, "band", "dom")),
        check_vma=False,
    )
```
